512 devices in a mesh: grid: 128 (over z, y, x_hi), chan: 4 (over x_lo, core).
Axes of the slice: x: 4 (x_hi: 2, x_lo: 2; x = x_hi * 2 + x_lo), y: 8, z: 8, core: 2. Of those that a mesh axis runs over, the one named last changes fastest.
Arguments:
- field: bfloat16 [16, 1024, 768], P(None, 'grid', 'chan'), may hold values from -6 to 6
- cotangent: bfloat16 [16, 1024, 768], P(None, 'grid', 'chan'), may hold values from -8.4 to 8.4
- pre_hidden: bfloat16 [16, 1024, 3072], P(None, 'grid', 'chan'), may hold values from -6 to 6
- w_up: bfloat16 [768, 3072], P(None, 'chan'), may hold values from -0.21875 to 0.21875
- w_down: bfloat16 [3072, 768], P('chan'), may hold values from -0.109375 to 0.109375
- gain: float32 [768], P('chan'), may hold values from 0.25 to 1.75
- tap_weights: float32 [20, 768], P(None, 'chan'), may hold values from -12 to 12
- basis: float32 [16, 20], replicated, may hold values from 0.05 to 0.5
- lon_offsets: int32 [16, 20], replicated, may hold values from -8 to 8, as said below
Outputs:
- field_grad: bfloat16 [16, 1024, 768], P(None, 'grid', 'chan')
- gain_grad: float32 [768], P('chan')
- tap_grad: float32 [20, 768], P(None, 'chan')
The draws below stay inside these ranges and needn't reach their ends.
Inputs may be any that keep to these rules, and one draw needn't show every extreme that they name: `lon_offsets`: both ends of the range are reached in every draw.
All inputs are finite; a program needn't handle non-finite values.
Results may differ from the reference program's by a relative error of at most 0.005.
Values may be sent and summed in bfloat16 or wider, within the bound.
No kernel may reach another device: no remote copies, remote signals or barrier semaphores. Data moves between devices by JAX's collectives and lax.ppermute only.
A program may use at most 64 MiB of HBM per device.

```python
import math
import jax
import jax.numpy as jnp
from jax import lax

D = 768
FF = 3072
ROWS = 16
HALO = 8
REACH = 2
PER_ROW = 4
TAPS = 20
NLON = 1024


def draw_lon_offsets(key, part):
    table_key, east_key, west_key = jax.random.split(key, 3)
    table = jax.random.randint(table_key, (ROWS, TAPS), -HALO, HALO + 1)
    east_row = jax.random.randint(east_key, (), 0, ROWS)
    west_row = jax.random.randint(west_key, (), 0, ROWS)
    table = table.at[east_row, 0].set(HALO)
    table = table.at[west_row, 1].set(-HALO)
    return table.astype(jnp.int32)


def draw_tap_weights(key, part):
    channel_ramp = jnp.exp(jnp.log(3.0) * jnp.arange(D, dtype=jnp.float32) / D)
    values = jax.random.normal(key, (TAPS, D), jnp.float32)
    values = jnp.clip(values, -4.0, 4.0)
    return values * channel_ramp[None, :]


def draw_cotangent(key, part):
    lon_ramp = jnp.exp(jnp.log(3.0) * jnp.arange(NLON, dtype=jnp.float32) / NLON)
    base_key = jax.random.fold_in(key, 0)
    values = jax.random.normal(base_key, (ROWS, NLON, D), jnp.float32)
    values = jnp.clip(values, -4.0, 4.0)
    return (values * lon_ramp[None, :, None] * 0.7).astype(jnp.bfloat16)


def level_of(stream_key, extent, shards, smallest, largest):
    level, own = 1.0, jax.random.fold_in(stream_key, 6)
    for axis_at, blocks in shards:
        steps = jnp.exp(jax.random.uniform(jax.random.fold_in(own, axis_at), (blocks,), jnp.float32, smallest / len(shards), largest / len(shards)))
        level = level * jnp.repeat(steps, extent[axis_at] // blocks).reshape([-1 if axis == axis_at else 1 for axis in range(len(extent))])
    return level


def scatter_about(own_key, shape, spread, bound, cuts=(), kind=jnp.bfloat16):
    result = spread * jax.random.normal(own_key, shape, jnp.float32)
    if cuts:
        result = result * level_of(own_key, shape, cuts, -0.22, 0.18)
    return jnp.clip(result, -bound, bound).astype(kind)


def setup_inputs(seed: int = 0) -> dict:
    seeds = jax.random.split(jax.random.key(seed), 10)
    return {
        "field": scatter_about(seeds[0], (ROWS, NLON, D), 1.0, 6.0, ((1, 128), (2, 4))),
        "cotangent": draw_cotangent(jax.random.fold_in(seeds[9], 71), 0),
        "pre_hidden": scatter_about(seeds[2], (ROWS, NLON, FF), 1.5, 6.0, ((1, 128), (2, 4))),
        "w_up": scatter_about(seeds[3], (D, FF), D ** -0.5, 0.21875, ((1, 4),)),
        "w_down": scatter_about(seeds[4], (FF, D), FF ** -0.5, 0.109375, ((0, 4),)),
        "gain": jnp.clip(1.0 + 0.15 * jax.random.normal(seeds[5], (D,), jnp.float32), 0.25, 1.75),
        "tap_weights": draw_tap_weights(jax.random.fold_in(seeds[9], 71), 0),
        "basis": jnp.clip(jnp.exp(jax.random.uniform(seeds[7], (ROWS, TAPS), jnp.float32, math.log(0.05), math.log(0.5))), 0.05, 0.5),
        "lon_offsets": draw_lon_offsets(jax.random.fold_in(seeds[9], 71), 0),
    }


EPSILON = 1e-05
INV_SQRT_TWO = 0.7071067811865476
INV_SQRT_TWO_PI = 0.3989422804014327

def tap_indices(row_step, lon_step):
    source_rows = jnp.arange(ROWS, dtype=jnp.int32) + row_step
    inside = ((source_rows >= 0) & (source_rows < ROWS)).astype(jnp.float32)
    clipped = jnp.clip(source_rows, 0, ROWS - 1).astype(jnp.int32)
    columns = (jnp.arange(NLON, dtype=jnp.int32)[None, :] + lon_step[:, None]) % NLON
    return (clipped, columns.astype(jnp.int32), inside)

def reference(field, cotangent, pre_hidden, w_up, w_down, gain, tap_weights, basis, lon_offsets):
    row_steps = (jnp.arange(TAPS, dtype=jnp.int32) // PER_ROW - REACH).astype(jnp.int32)
    tap_items = (row_steps, lon_offsets.T, basis.T, tap_weights)

    def forward_step(running, item):
        row_step, lon_step, basis_col, weight_row = item
        clipped, columns, inside = tap_indices(row_step, lon_step)
        picked = field[clipped[:, None], columns].astype(jnp.float32)
        coefficient = basis_col[:, None] * weight_row[None, :]
        return (running + coefficient[:, None, :] * picked * inside[:, None, None], None)
    forward = lax.scan(forward_step, jnp.zeros((ROWS, NLON, D), jnp.float32), tap_items)[0]
    inv_rms = lax.rsqrt(lax.optimization_barrier(jnp.mean(forward * forward, axis=-1)) + EPSILON)

    def row_backward(item):
        cot_row, pre_row = item
        hidden_grad = jnp.dot(cot_row, w_down.T, preferred_element_type=jnp.float32)
        pre_value = pre_row.astype(jnp.float32)
        slope = 0.5 * (1.0 + lax.erf(pre_value * INV_SQRT_TWO)) + pre_value * jnp.exp(-0.5 * pre_value * pre_value) * INV_SQRT_TWO_PI
        pre_grad = (hidden_grad * slope).astype(jnp.bfloat16)
        return jnp.dot(pre_grad, w_up.T, preferred_element_type=jnp.float32)
    norm_grad = lax.map(row_backward, (cotangent, pre_hidden))
    scaled = gain * norm_grad
    inner = lax.optimization_barrier(jnp.mean(forward * scaled, axis=-1))
    field_term = inv_rms[..., None] * scaled - forward * (inv_rms ** 3 * inner)[..., None]
    scale_sum = 1.0 / jnp.sqrt(jnp.float32(ROWS * NLON))
    gain_grad = lax.optimization_barrier(jnp.sum(norm_grad * forward * inv_rms[..., None], axis=(0, 1))) * scale_sum

    def adjoint_step(running, item):
        row_step, lon_step, basis_col, weight_row = item
        clipped, columns, inside = tap_indices(row_step, lon_step)
        picked = field[clipped[:, None], columns].astype(jnp.float32)
        coefficient = basis_col[:, None] * weight_row[None, :]
        contrib = coefficient[:, None, :] * field_term * inside[:, None, None]
        running = running.at[clipped[:, None], columns].add(contrib)
        tap_row = lax.optimization_barrier(jnp.sum(basis_col[:, None, None] * field_term * picked * inside[:, None, None], axis=(0, 1)))
        return (running, tap_row)
    adjoint, tap_rows = lax.scan(adjoint_step, jnp.zeros((ROWS, NLON, D), jnp.float32), tap_items)
    field_grad = (cotangent.astype(jnp.float32) + adjoint).astype(jnp.bfloat16)
    return (field_grad, gain_grad, tap_rows * scale_sum)
```

```python
import math

import jax
import jax.numpy as jnp
from jax import lax
from jax.experimental import pallas as pl
from jax.experimental.pallas import tpu as pltpu
from jax.sharding import Mesh
from jax.sharding import PartitionSpec as P

ROWS = 16
LON = 8
CELLS = ROWS * LON
D = 768
CH = 192
HID = 768
TAPS = 20
REACH = 2
PER_ROW = 4
NCHAN = 4
EXT = 3 * LON
GRID = ("z", "y", "xh")

EPSILON = 1e-05
INV_SQRT_TWO = 0.7071067811865476
INV_SQRT_TWO_PI = 0.3989422804014327
SCALE = 1.0 / math.sqrt(16384.0)

F32 = jnp.float32
BF16 = jnp.bfloat16
NT = (((1,), (1,)), ((), ()))

SEND = 5 * CELLS + 16
PACK = 32
HALF = 11


def params():
    return pltpu.CompilerParams(vmem_limit_bytes=24 * 1024 * 1024)


VMEM = pl.BlockSpec(memory_space=pltpu.VMEM)
SMEM = pl.BlockSpec(memory_space=pltpu.SMEM)


def taps_from(row):
    out = []
    for k in range(TAPS):
        src = row + k // PER_ROW - REACH
        if 0 <= src < ROWS:
            out.append((k, src))
    return out


def fill_ext(ext, left, own, right):
    ext[1] = jnp.zeros((ROWS * EXT, 128), F32)
    for at, ref in enumerate((left, own, right)):
        v = ref[...].astype(F32)
        for r in range(ROWS):
            to = pl.ds(EXT * r + LON * at, LON)
            ext[0, to, :] = v[LON * r : LON * r + LON, :128]
            ext[1, to, : CH - 128] = v[LON * r : LON * r + LON, 128:]


def mlp_kernel(cot, pre, w_down, w_up, out, cot_all):
    for i in range(NCHAN):
        cot_all[:, CH * i : CH * (i + 1)] = cot[i]
    hidden = lax.dot_general(cot_all[...], w_down[...], NT, preferred_element_type=F32)
    v = pre[...].astype(F32)
    slope = (
        0.5 * (1.0 + lax.erf(v * INV_SQRT_TWO))
        + v * jnp.exp(-0.5 * v * v) * INV_SQRT_TWO_PI
    )
    grad = (hidden * slope).astype(BF16)
    for i in range(NCHAN):
        part = lax.dot_general(
            grad, w_up[CH * i : CH * (i + 1), :], NT, preferred_element_type=F32
        )
        out[CELLS * i : CELLS * (i + 1), :] = part.astype(BF16)


def forward_kernel(offs, basis, left, own, right, taps, gain, part, fwd, send, ext):
    fill_ext(ext, left, own, right)
    for r in range(ROWS):
        lo = jnp.zeros((LON, 128), F32)
        hi = jnp.zeros((LON, 128), F32)
        for k, src in taps_from(r):
            at = pl.ds(EXT * src + LON + offs[r, k], LON)
            lo += basis[r, k] * (taps[k : k + 1, :128] * ext[0, at, :])
            hi += basis[r, k] * (taps[k : k + 1, 128:] * ext[1, at, :])
        fwd[LON * r : LON * (r + 1), :128] = lo
        fwd[LON * r : LON * (r + 1), 128:] = hi[:, : CH - 128]
    send[: 4 * CELLS, :] = part[...]
    send[4 * CELLS : 5 * CELLS, :] = fwd[...].astype(BF16)
    g = gain[...]
    top = g.astype(BF16)
    mid = (g - top.astype(F32)).astype(BF16)
    low = (g - top.astype(F32) - mid.astype(F32)).astype(BF16)
    row = lax.broadcasted_iota(jnp.int32, (16, CH), 0)
    wide = jnp.where(row == 0, top.astype(F32), jnp.where(row == 1, mid.astype(F32), low.astype(F32)))
    send[5 * CELLS :, :] = wide.astype(BF16)


def term_kernel(me, offs, basis, left, own, right, fwd, got, term, term16, packed, ext, rows):
    fill_ext(ext, left, own, right)
    squares = jnp.zeros((CELLS, 1), F32)
    inner = jnp.zeros((CELLS, 1), F32)
    for j in range(NCHAN):
        norm = got[0, CELLS * j : CELLS * (j + 1), :].astype(F32)
        for h in range(1, NCHAN):
            norm += got[h, CELLS * j : CELLS * (j + 1), :].astype(F32)
        f = got[j, 4 * CELLS : 5 * CELLS, :].astype(F32)
        g3 = got[j, 5 * CELLS :, :].astype(F32)
        g = g3[0:1] + g3[1:2] + g3[2:3]
        squares += jnp.sum(f * f, axis=1, keepdims=True)
        inner += jnp.sum(f * (g * norm), axis=1, keepdims=True)
    mine = pl.ds(pl.multiple_of(me[0] * CELLS, CELLS), CELLS)
    norm = got[0, mine, :].astype(F32)
    for h in range(1, NCHAN):
        norm += got[h, mine, :].astype(F32)
    g3 = got[me[0], 5 * CELLS :, :].astype(F32)
    g = g3[0:1] + g3[1:2] + g3[2:3]
    inv_rms = lax.rsqrt(squares / D + EPSILON)
    f = fwd[...]
    ft = inv_rms * (g * norm) - f * (inv_rms * inv_rms * inv_rms * (inner / D))
    term[...] = ft
    term16[...] = ft.astype(BF16)
    gain_row = jnp.sum(norm * f * inv_rms, axis=0, keepdims=True)
    rows[...] = jnp.zeros((2, 24, 128), F32)
    rows[0, 20:21, :] = gain_row[:, :128]
    rows[1, 20:21, : CH - 128] = gain_row[:, 128:]
    pad = jnp.zeros((LON, 256 - CH), F32)
    for k in range(TAPS):
        lo = jnp.zeros((LON, 128), F32)
        hi = jnp.zeros((LON, 128), F32)
        for r in range(ROWS):
            src = r + k // PER_ROW - REACH
            if 0 <= src < ROWS:
                at = pl.ds(EXT * src + LON + offs[r, k], LON)
                lo += basis[r, k] * (ft[LON * r : LON * (r + 1), :128] * ext[0, at, :])
                wide = jnp.concatenate([ft[LON * r : LON * (r + 1), 128:], pad], axis=1)
                hi += basis[r, k] * (wide * ext[1, at, :])
        rows[0, k : k + 1, :] = jnp.sum(lo, axis=0, keepdims=True)
        rows[1, k : k + 1, :] = jnp.sum(hi, axis=0, keepdims=True)
    first = rows[0, 0:21, :]
    second = rows[1, 0:HALF, :] + pltpu.roll(rows[1, HALF : 2 * HALF, :], 64, 1)
    value = jnp.concatenate([first, second], axis=0).astype(BF16)
    for i in range(8):
        packed[i] = value


def sum_kernel(got, out):
    total = got[0].astype(F32)
    for i in range(1, 8):
        total += got[i].astype(F32)
    total = total.astype(BF16)
    for i in range(16):
        out[i] = total


def final_kernel(offs, basis, left, term, right, taps, cot, got, grad, gain_grad, tap_grad, ext, total):
    fill_ext(ext, left, term, right)
    for r2 in range(ROWS):
        lo = jnp.zeros((LON, 128), F32)
        hi = jnp.zeros((LON, 128), F32)
        for k in range(TAPS):
            r = r2 - (k // PER_ROW - REACH)
            if 0 <= r < ROWS:
                at = pl.ds(EXT * r + LON - offs[r, k], LON)
                lo += basis[r, k] * (taps[k : k + 1, :128] * ext[0, at, :])
                hi += basis[r, k] * (taps[k : k + 1, 128:] * ext[1, at, :])
        total[LON * r2 : LON * (r2 + 1), :128] = lo
        total[LON * r2 : LON * (r2 + 1), 128:] = hi[:, : CH - 128]
    grad[...] = (cot[...].astype(F32) + total[...]).astype(BF16)
    value = got[0].astype(F32)
    for i in range(1, 16):
        value += got[i].astype(F32)
    value = value * SCALE
    tap_grad[:, :128] = value[0:TAPS]
    gain_grad[:, :128] = value[TAPS : TAPS + 1]
    back = pltpu.roll(value[21:32], 64, 1)
    tap_grad[0:HALF, 128:] = value[21:32, : CH - 128]
    tap_grad[HALF:TAPS, 128:] = back[0 : TAPS - HALF, : CH - 128]
    gain_grad[:, 128:] = back[TAPS - HALF : TAPS - HALF + 1, : CH - 128]


def shape(dims, dtype=F32):
    return jax.ShapeDtypeStruct(dims, dtype)


def both_ways(value):
    n = 128
    left = lax.ppermute(value, GRID, [(i, (i + 1) % n) for i in range(n)])
    right = lax.ppermute(value, GRID, [(i, (i - 1) % n) for i in range(n)])
    return left, right


def per_device(field, cotangent, pre_hidden, w_up, w_down, gain, tap_weights, basis, lon_offsets):
    field = field.reshape(CELLS, CH)
    cot = cotangent.reshape(CELLS, CH)
    pre = pre_hidden.reshape(CELLS, HID)
    taps = jnp.pad(tap_weights, ((0, 0), (0, 256 - CH)))
    me = lax.axis_index("chan").astype(jnp.int32).reshape(1)
    left, right = both_ways(field)
    cot_all = lax.all_gather(cot, "chan")
    part = pl.pallas_call(
        mlp_kernel,
        out_shape=shape((4 * CELLS, CH), BF16),
        in_specs=[VMEM] * 4,
        out_specs=VMEM,
        scratch_shapes=[pltpu.VMEM((CELLS, D), BF16)],
        compiler_params=params(),
        name="mlp",
    )(cot_all, pre, w_down, w_up)
    fwd, send = pl.pallas_call(
        forward_kernel,
        out_shape=(shape((CELLS, CH)), shape((SEND, CH), BF16)),
        in_specs=[SMEM, SMEM] + [VMEM] * 6,
        out_specs=(VMEM, VMEM),
        scratch_shapes=[pltpu.VMEM((2, ROWS * EXT, 128), F32)],
        compiler_params=params(),
        name="forward",
    )(lon_offsets, basis, left, field, right, taps, gain.reshape(1, CH), part)
    got = lax.all_gather(send, "chan")
    term, term16, packed = pl.pallas_call(
        term_kernel,
        out_shape=(shape((CELLS, CH)), shape((CELLS, CH), BF16), shape((8, PACK, 128), BF16)),
        in_specs=[SMEM] * 3 + [VMEM] * 5,
        out_specs=(VMEM,) * 3,
        scratch_shapes=[pltpu.VMEM((2, ROWS * EXT, 128), F32), pltpu.VMEM((2, 24, 128), F32)],
        compiler_params=params(),
        name="term",
    )(me, lon_offsets, basis, left, field, right, fwd, got)
    term_left, term_right = both_ways(term16)
    over_z = lax.all_to_all(packed, "z", 0, 0)
    again = pl.pallas_call(
        sum_kernel,
        out_shape=shape((16, PACK, 128), BF16),
        in_specs=[VMEM],
        out_specs=VMEM,
        compiler_params=params(),
        name="zsum",
    )(over_z)
    over_yx = lax.all_to_all(again, ("y", "xh"), 0, 0)
    grad, gain_grad, tap_grad = pl.pallas_call(
        final_kernel,
        out_shape=(shape((CELLS, CH), BF16), shape((1, CH)), shape((TAPS, CH))),
        in_specs=[SMEM, SMEM] + [VMEM] * 6,
        out_specs=(VMEM,) * 3,
        scratch_shapes=[pltpu.VMEM((2, ROWS * EXT, 128), F32), pltpu.VMEM((CELLS, CH), F32)],
        compiler_params=params(),
        name="final",
    )(lon_offsets, basis, term_left, term, term_right, taps, cot, over_yx)
    return (grad.reshape(ROWS, LON, CH), gain_grad.reshape(CH), tap_grad)


def solution(mesh):
    fine = Mesh(mesh.devices.reshape(8, 8, 2, NCHAN), (*GRID, "chan"))
    cells = P(None, GRID, "chan")
    placed = (
        cells,
        cells,
        cells,
        P(None, "chan"),
        P("chan", None),
        P("chan"),
        P(None, "chan"),
        P(),
        P(),
    )
    return jax.shard_map(
        per_device,
        mesh=fine,
        in_specs=placed,
        out_specs=(cells, P("chan"), P(None, "chan")),
        check_vma=False,
    )
```

```python
import math

import jax
import jax.numpy as jnp
from jax import lax
from jax.experimental import pallas as pl
from jax.experimental.pallas import tpu as pltpu
from jax.sharding import Mesh
from jax.sharding import PartitionSpec as P

ROWS = 16
LON = 8
CELLS = ROWS * LON
D = 768
CH = 192
HID = 768
TAPS = 20
REACH = 2
PER_ROW = 4
NCHAN = 4
EXT = 3 * LON
GRID = ("z", "y", "xh")

EPSILON = 1e-05
INV_SQRT_TWO = 0.7071067811865476
INV_SQRT_TWO_PI = 0.3989422804014327
SCALE = 1.0 / math.sqrt(16384.0)

F32 = jnp.float32
BF16 = jnp.bfloat16
NT = (((1,), (1,)), ((), ()))

FWD_AT = D
SQ_AT = D + CH
SEND = SQ_AT + 16
PACK = 32
HALF = 11

VMEM = pl.BlockSpec(memory_space=pltpu.VMEM)
SMEM = pl.BlockSpec(memory_space=pltpu.SMEM)
HBM = pl.BlockSpec(memory_space=pltpu.HBM)


def call(kernel, outs, ins, out_specs, scratch, name, flops=0, moved=0, limit=24):
    return pl.pallas_call(
        kernel,
        out_shape=outs,
        in_specs=ins,
        out_specs=out_specs,
        scratch_shapes=scratch,
        compiler_params=pltpu.CompilerParams(vmem_limit_bytes=limit * 1024 * 1024),
        cost_estimate=pl.CostEstimate(flops=flops, bytes_accessed=moved, transcendentals=0),
        name=name,
    )


def taps_from(row):
    out = []
    for k in range(TAPS):
        src = row + k // PER_ROW - REACH
        if 0 <= src < ROWS:
            out.append((k, src))
    return out


def fill_own(ext, ref):
    v = ref[...].astype(F32)
    for r in range(ROWS):
        to = pl.ds(EXT * r + LON, LON)
        ext[0, to, :] = v[LON * r : LON * r + LON, :128]
        ext[1, to, : CH - 128] = v[LON * r : LON * r + LON, 128:]


def fill_side(ext, ref, start):
    v = ref[...].astype(F32)
    for r in range(ROWS):
        to = pl.ds(pl.multiple_of(EXT * r + start, LON), LON)
        ext[0, to, :] = v[LON * r : LON * r + LON, :128]
        ext[1, to, : CH - 128] = v[LON * r : LON * r + LON, 128:]


def fill_ext(ext, place, own, near, far):
    ext[1] = jnp.zeros((ROWS * EXT, 128), F32)
    start = 2 * LON * (1 - (place[0] >> 2))
    fill_own(ext, own)
    fill_side(ext, near, start)
    fill_side(ext, far, 2 * LON - start)


def prep_kernel(cot, out):
    turned = cot[...].astype(F32).T.astype(BF16)
    for i in range(NCHAN):
        out[i] = turned


def ready_kernel(pre, gain, taps, slope, gain_t, wide):
    v = pre[...].astype(F32)
    s = (
        0.5 * (1.0 + lax.erf(v * INV_SQRT_TWO))
        + v * jnp.exp(-0.5 * v * v) * INV_SQRT_TWO_PI
    )
    slope[...] = s.T
    gain_t[...] = jnp.broadcast_to(gain[...], (CELLS, CH)).T
    wide[...] = jnp.zeros((TAPS, 256), F32)
    wide[:, :CH] = taps[...]


def mlp_kernel(cot, slope, down, up, out):
    hidden = jnp.dot(down[...], cot[...], preferred_element_type=F32)
    grad = (hidden * slope[...]).astype(BF16)
    out[...] = jnp.dot(up[...], grad, preferred_element_type=F32).astype(BF16)


def forward_kernel(place, offs, basis, own, near, far, taps, gain_t, part, fwd_t, send, ext, fwd):
    fill_ext(ext, place, own, near, far)
    for r in range(ROWS):
        lo = jnp.zeros((LON, 128), F32)
        hi = jnp.zeros((LON, 128), F32)
        for k, src in taps_from(r):
            at = pl.ds(EXT * src + LON + offs[r, k], LON)
            lo += basis[r, k] * (taps[k : k + 1, :128] * ext[0, at, :])
            hi += basis[r, k] * (taps[k : k + 1, 128:] * ext[1, at, :])
        fwd[LON * r : LON * (r + 1), :128] = lo
        fwd[LON * r : LON * (r + 1), 128:] = hi[:, : CH - 128]
    f = fwd[...].T
    fwd_t[...] = f
    send[:FWD_AT, :] = part[...]
    send[FWD_AT:SQ_AT, :] = (gain_t[...] * f).astype(BF16)
    sq = jnp.sum(f * f, axis=0, keepdims=True)
    top = sq.astype(BF16).astype(F32)
    mid = (sq - top).astype(BF16).astype(F32)
    row = lax.broadcasted_iota(jnp.int32, (16, CELLS), 0)
    three = jnp.where(row == 0, top, jnp.where(row == 1, mid, sq - top - mid))
    send[SQ_AT:, :] = three.astype(BF16)


def term_kernel(place, offs, basis, ext, fwd_t, gain_t, got, term, term16, packed, rows):
    inner = jnp.zeros((1, CELLS), F32)
    squares = jnp.zeros((1, CELLS), F32)
    for j in range(NCHAN):
        norm = got[0, CH * j : CH * (j + 1), :].astype(F32)
        for h in range(1, NCHAN):
            norm += got[h, CH * j : CH * (j + 1), :].astype(F32)
        f = got[j, FWD_AT:SQ_AT, :].astype(F32)
        inner += jnp.sum(f * norm, axis=0, keepdims=True)
        three = got[j, SQ_AT:, :].astype(F32)
        squares += three[0:1] + three[1:2] + three[2:3]
    mine = pl.ds(pl.multiple_of((place[0] & 3) * CH, CH), CH)
    norm = got[0, mine, :].astype(F32)
    for h in range(1, NCHAN):
        norm += got[h, mine, :].astype(F32)
    inv_rms = lax.rsqrt(squares / D + EPSILON)
    f = fwd_t[...]
    scaled = inv_rms * norm
    ft = (gain_t[...] * scaled - f * (inv_rms * inv_rms * inv_rms * (inner / D))).T
    term[...] = ft
    term16[...] = ft.astype(BF16)
    gain_row = jnp.sum((scaled * f).T, axis=0, keepdims=True)
    rows[...] = jnp.zeros((2, 24, 128), F32)
    rows[0, 20:21, :] = gain_row[:, :128]
    rows[1, 20:21, : CH - 128] = gain_row[:, 128:]
    pad = jnp.zeros((LON, 256 - CH), F32)
    for k in range(TAPS):
        lo = jnp.zeros((LON, 128), F32)
        hi = jnp.zeros((LON, 128), F32)
        for r in range(ROWS):
            src = r + k // PER_ROW - REACH
            if 0 <= src < ROWS:
                at = pl.ds(EXT * src + LON + offs[r, k], LON)
                lo += basis[r, k] * (ft[LON * r : LON * (r + 1), :128] * ext[0, at, :])
                wide = jnp.concatenate([ft[LON * r : LON * (r + 1), 128:], pad], axis=1)
                hi += basis[r, k] * (wide * ext[1, at, :])
        rows[0, k : k + 1, :] = jnp.sum(lo, axis=0, keepdims=True)
        rows[1, k : k + 1, :] = jnp.sum(hi, axis=0, keepdims=True)
    first = rows[0, 0:21, :]
    second = rows[1, 0:HALF, :] + pltpu.roll(rows[1, HALF : 2 * HALF, :], 64, 1)
    value = jnp.concatenate([first, second], axis=0).astype(BF16)
    for i in range(16):
        packed[i] = value


def resum_kernel(got, out):
    total = got[0].astype(F32)
    for i in range(1, 16):
        total += got[i].astype(F32)
    total = total.astype(BF16)
    for i in range(8):
        out[i] = total


def adjoint_kernel(place, offs, basis, own, near, far, taps, cot, grad, ext, total):
    fill_ext(ext, place, own, near, far)
    for r2 in range(ROWS):
        lo = jnp.zeros((LON, 128), F32)
        hi = jnp.zeros((LON, 128), F32)
        for k in range(TAPS):
            r = r2 - (k // PER_ROW - REACH)
            if 0 <= r < ROWS:
                at = pl.ds(EXT * r + LON - offs[r, k], LON)
                lo += basis[r, k] * (taps[k : k + 1, :128] * ext[0, at, :])
                hi += basis[r, k] * (taps[k : k + 1, 128:] * ext[1, at, :])
        total[LON * r2 : LON * (r2 + 1), :128] = lo
        total[LON * r2 : LON * (r2 + 1), 128:] = hi[:, : CH - 128]
    grad[...] = (cot[...].astype(F32) + total[...]).astype(BF16)


def last_kernel(got, gain_grad, tap_grad):
    value = got[0].astype(F32)
    for i in range(1, 8):
        value += got[i].astype(F32)
    value = value * SCALE
    tap_grad[:, :128] = value[0:TAPS]
    gain_grad[:, :128] = value[TAPS : TAPS + 1]
    back = pltpu.roll(value[21:32], 64, 1)
    tap_grad[0:HALF, 128:] = value[21:32, : CH - 128]
    tap_grad[HALF:TAPS, 128:] = back[0 : TAPS - HALF, : CH - 128]
    gain_grad[:, 128:] = back[TAPS - HALF : TAPS - HALF + 1, : CH - 128]


def shape(dims, dtype=F32):
    return jax.ShapeDtypeStruct(dims, dtype)


def swap_near(value):
    return lax.ppermute(value, "xh", [(0, 1), (1, 0)])


def swap_far(value):
    n = 128
    return lax.ppermute(value, GRID, [(i, (i + 1 if i % 2 else i - 1) % n) for i in range(n)])


def per_device(field, cotangent, pre_hidden, w_up, w_down, gain, tap_weights, basis, lon_offsets):
    field = field.reshape(CELLS, CH)
    cot = cotangent.reshape(CELLS, CH)
    pre = pre_hidden.reshape(CELLS, HID)
    place = lax.axis_index(("xh", "chan")).astype(jnp.int32).reshape(1)
    ext_shape = (2, ROWS * EXT, 128)

    cots = call(prep_kernel, shape((NCHAN, CH, CELLS), BF16), [VMEM], VMEM, [], "prep", flops=8_000_000_000)(cot)
    cot_all = lax.all_to_all(cots, "chan", 0, 0).reshape(D, CELLS)
    near, far = swap_near(field), swap_far(field)
    slope, gain_t, taps = call(
        ready_kernel,
        (shape((HID, CELLS)), shape((CH, CELLS)), shape((TAPS, 256))),
        [VMEM] * 3,
        (VMEM,) * 3,
        [],
        "ready",
        moved=3_000_000,
    )(pre, gain.reshape(1, CH), tap_weights)
    part = call(mlp_kernel, shape((D, CELLS), BF16), [VMEM] * 4, VMEM, [], "mlp", flops=300_000_000)(
        cot_all, slope, w_down, w_up
    )
    fwd_t, send, ext = call(
        forward_kernel,
        (shape((CH, CELLS)), shape((SEND, CELLS), BF16), shape(ext_shape)),
        [SMEM] * 3 + [VMEM] * 6,
        (VMEM,) * 3,
        [pltpu.VMEM((CELLS, CH), F32)],
        "forward",
    )(place, lon_offsets, basis, field, near, far, taps, gain_t, part)
    got = lax.all_gather(send, "chan")
    term, term16, packed = call(
        term_kernel,
        (shape((CELLS, CH)), shape((CELLS, CH), BF16), shape((16, PACK, 128), BF16)),
        [SMEM] * 3 + [VMEM] * 4,
        (VMEM,) * 3,
        [pltpu.VMEM((2, 24, 128), F32)],
        "term",
    )(place, lon_offsets, basis, ext, fwd_t, gain_t, got)
    over_yx = lax.all_to_all(packed, ("y", "xh"), 0, 0)
    term_far = swap_far(term16)
    over_yx, term_far, term_again = lax.optimization_barrier((over_yx, term_far, term16))
    again = call(resum_kernel, shape((8, PACK, 128), BF16), [VMEM], VMEM, [], "resum")(over_yx)
    over_z = lax.all_to_all(again, "z", 0, 0)
    term_near = swap_near(term_again)
    grad = call(
        adjoint_kernel,
        shape((CELLS, CH), BF16),
        [SMEM] * 3 + [VMEM] * 5,
        VMEM,
        [pltpu.VMEM(ext_shape, F32), pltpu.VMEM((CELLS, CH), F32)],
        "adjoint",
        moved=6_000_000,
    )(place, lon_offsets, basis, term, term_near, term_far, taps, cot)
    gain_grad, tap_grad = call(
        last_kernel, (shape((1, CH)), shape((TAPS, CH))), [VMEM], (VMEM,) * 2, [], "last"
    )(over_z)
    return (grad.reshape(ROWS, LON, CH), gain_grad.reshape(CH), tap_grad)


def solution(mesh):
    fine = Mesh(mesh.devices.reshape(8, 8, 2, NCHAN), (*GRID, "chan"))
    cells = P(None, GRID, "chan")
    placed = (
        cells,
        cells,
        cells,
        P(None, "chan"),
        P("chan", None),
        P("chan"),
        P(None, "chan"),
        P(),
        P(),
    )
    return jax.shard_map(
        per_device,
        mesh=fine,
        in_specs=placed,
        out_specs=(cells, P("chan"), P(None, "chan")),
        check_vma=False,
    )
```

```python
import math

import jax
import jax.numpy as jnp
from jax import lax
from jax.experimental import pallas as pl
from jax.experimental.pallas import tpu as pltpu
from jax.sharding import Mesh
from jax.sharding import PartitionSpec as P

ROWS = 16
LON = 8
CELLS = ROWS * LON
D = 768
CH = 192
HID = 768
TAPS = 20
REACH = 2
PER_ROW = 4
NCHAN = 4
EXT = 3 * LON
GRID = ("z", "y", "xh")

EPSILON = 1e-05
INV_SQRT_TWO = 0.7071067811865476
INV_SQRT_TWO_PI = 0.3989422804014327
SCALE = 1.0 / math.sqrt(16384.0)

F32 = jnp.float32
BF16 = jnp.bfloat16
NT = (((1,), (1,)), ((), ()))

FWD_AT = D
SQ_AT = D + CH
SEND = SQ_AT + 16
PACK = 32
HALF = 11

VMEM = pl.BlockSpec(memory_space=pltpu.VMEM)
SMEM = pl.BlockSpec(memory_space=pltpu.SMEM)
HBM = pl.BlockSpec(memory_space=pltpu.HBM)


def call(kernel, outs, ins, out_specs, scratch, name, flops=0, moved=0, limit=24):
    return pl.pallas_call(
        kernel,
        out_shape=outs,
        in_specs=ins,
        out_specs=out_specs,
        scratch_shapes=scratch,
        compiler_params=pltpu.CompilerParams(vmem_limit_bytes=limit * 1024 * 1024),
        cost_estimate=pl.CostEstimate(flops=flops, bytes_accessed=moved, transcendentals=0),
        name=name,
    )


def taps_from(row):
    out = []
    for k in range(TAPS):
        src = row + k // PER_ROW - REACH
        if 0 <= src < ROWS:
            out.append((k, src))
    return out


def fill_own(ext, v):
    for r in range(ROWS):
        to = pl.ds(EXT * r + LON, LON)
        ext[0, to, :] = v[LON * r : LON * r + LON, :128]
        ext[1, to, : CH - 128] = v[LON * r : LON * r + LON, 128:]


def fill_side(ext, v, start):
    for r in range(ROWS):
        to = pl.ds(pl.multiple_of(EXT * r + start, LON), LON)
        ext[0, to, :] = v[LON * r : LON * r + LON, :128]
        ext[1, to, : CH - 128] = v[LON * r : LON * r + LON, 128:]


def fill_ext(ext, place, own, near, far):
    ext[1] = jnp.zeros((ROWS * EXT, 128), F32)
    start = 2 * LON * (1 - (place[0] >> 2))
    fill_own(ext, own)
    fill_side(ext, near, start)
    fill_side(ext, far, 2 * LON - start)


def prep_kernel(place, cot, field, out):
    cot_t = cot[...].astype(F32).T.astype(BF16)
    field_t = field[...].astype(F32).T.astype(BF16)
    x_hi = place[0] >> 2
    for i in range(NCHAN):
        out[NCHAN * x_hi + i] = cot_t
        out[NCHAN * (1 - x_hi) + i] = field_t


def ready_kernel(pre, gain, taps, slope, gain_t, wide):
    v = pre[...].astype(F32)
    s = (
        0.5 * (1.0 + lax.erf(v * INV_SQRT_TWO))
        + v * jnp.exp(-0.5 * v * v) * INV_SQRT_TWO_PI
    )
    slope[...] = s.T
    gain_t[...] = jnp.broadcast_to(gain[...], (CELLS, CH)).T
    wide[...] = jnp.zeros((TAPS, 256), F32)
    wide[:, :CH] = taps[...]


def mlp_kernel(place, line, slope, down, up, out):
    cot = line[pl.ds(NCHAN * (place[0] >> 2), NCHAN)].reshape(D, CELLS)
    hidden = jnp.dot(down[...], cot, preferred_element_type=F32)
    grad = (hidden * slope[...]).astype(BF16)
    out[...] = jnp.dot(up[...], grad, preferred_element_type=F32).astype(BF16)


def forward_kernel(place, offs, basis, own, line, far, taps, gain_t, part, fwd_t, send, ext, fwd):
    x_hi = place[0] >> 2
    near = line[NCHAN * (1 - x_hi) + (place[0] & 3)].astype(F32).T
    fill_ext(ext, place, own[...].astype(F32), near, far[...].astype(F32))
    for r in range(ROWS):
        lo = jnp.zeros((LON, 128), F32)
        hi = jnp.zeros((LON, 128), F32)
        for k, src in taps_from(r):
            at = pl.ds(EXT * src + LON + offs[r, k], LON)
            lo += basis[r, k] * (taps[k : k + 1, :128] * ext[0, at, :])
            hi += basis[r, k] * (taps[k : k + 1, 128:] * ext[1, at, :])
        fwd[LON * r : LON * (r + 1), :128] = lo
        fwd[LON * r : LON * (r + 1), 128:] = hi[:, : CH - 128]
    f = fwd[...].T
    fwd_t[...] = f
    send[:FWD_AT, :] = part[...]
    send[FWD_AT:SQ_AT, :] = (gain_t[...] * f).astype(BF16)
    sq = jnp.sum(f * f, axis=0, keepdims=True)
    top = sq.astype(BF16).astype(F32)
    mid = (sq - top).astype(BF16).astype(F32)
    row = lax.broadcasted_iota(jnp.int32, (16, CELLS), 0)
    three = jnp.where(row == 0, top, jnp.where(row == 1, mid, sq - top - mid))
    send[SQ_AT:, :] = three.astype(BF16)


def term_kernel(place, offs, basis, ext, fwd_t, gain_t, got, term, term16, packed, rows):
    inner = jnp.zeros((1, CELLS), F32)
    squares = jnp.zeros((1, CELLS), F32)
    for j in range(NCHAN):
        norm = got[0, CH * j : CH * (j + 1), :].astype(F32)
        for h in range(1, NCHAN):
            norm += got[h, CH * j : CH * (j + 1), :].astype(F32)
        f = got[j, FWD_AT:SQ_AT, :].astype(F32)
        inner += jnp.sum(f * norm, axis=0, keepdims=True)
        three = got[j, SQ_AT:, :].astype(F32)
        squares += three[0:1] + three[1:2] + three[2:3]
    mine = pl.ds(pl.multiple_of((place[0] & 3) * CH, CH), CH)
    norm = got[0, mine, :].astype(F32)
    for h in range(1, NCHAN):
        norm += got[h, mine, :].astype(F32)
    inv_rms = lax.rsqrt(squares / D + EPSILON)
    f = fwd_t[...]
    scaled = inv_rms * norm
    ft = (gain_t[...] * scaled - f * (inv_rms * inv_rms * inv_rms * (inner / D))).T
    term[...] = ft
    term16[...] = ft.astype(BF16)
    gain_row = jnp.sum((scaled * f).T, axis=0, keepdims=True)
    rows[...] = jnp.zeros((2, 24, 128), F32)
    rows[0, 20:21, :] = gain_row[:, :128]
    rows[1, 20:21, : CH - 128] = gain_row[:, 128:]
    pad = jnp.zeros((LON, 256 - CH), F32)
    for k in range(TAPS):
        lo = jnp.zeros((LON, 128), F32)
        hi = jnp.zeros((LON, 128), F32)
        for r in range(ROWS):
            src = r + k // PER_ROW - REACH
            if 0 <= src < ROWS:
                at = pl.ds(EXT * src + LON + offs[r, k], LON)
                lo += basis[r, k] * (ft[LON * r : LON * (r + 1), :128] * ext[0, at, :])
                wide = jnp.concatenate([ft[LON * r : LON * (r + 1), 128:], pad], axis=1)
                hi += basis[r, k] * (wide * ext[1, at, :])
        rows[0, k : k + 1, :] = jnp.sum(lo, axis=0, keepdims=True)
        rows[1, k : k + 1, :] = jnp.sum(hi, axis=0, keepdims=True)
    first = rows[0, 0:21, :]
    second = rows[1, 0:HALF, :] + pltpu.roll(rows[1, HALF : 2 * HALF, :], 64, 1)
    value = jnp.concatenate([first, second], axis=0).astype(BF16)
    for i in range(8):
        packed[i] = value


def resum_kernel(got, out):
    total = got[0].astype(F32)
    for i in range(1, 8):
        total += got[i].astype(F32)
    total = total.astype(BF16)
    for i in range(16):
        out[i] = total


def adjoint_kernel(place, offs, basis, own, near, far, taps, cot, grad, ext, total):
    fill_ext(ext, place, own[...], near[...].astype(F32), far[...].astype(F32))
    for r2 in range(ROWS):
        lo = jnp.zeros((LON, 128), F32)
        hi = jnp.zeros((LON, 128), F32)
        for k in range(TAPS):
            r = r2 - (k // PER_ROW - REACH)
            if 0 <= r < ROWS:
                at = pl.ds(EXT * r + LON - offs[r, k], LON)
                lo += basis[r, k] * (taps[k : k + 1, :128] * ext[0, at, :])
                hi += basis[r, k] * (taps[k : k + 1, 128:] * ext[1, at, :])
        total[LON * r2 : LON * (r2 + 1), :128] = lo
        total[LON * r2 : LON * (r2 + 1), 128:] = hi[:, : CH - 128]
    grad[...] = (cot[...].astype(F32) + total[...]).astype(BF16)


def last_kernel(got, gain_grad, tap_grad):
    value = got[0].astype(F32)
    for i in range(1, 16):
        value += got[i].astype(F32)
    value = value * SCALE
    tap_grad[:, :128] = value[0:TAPS]
    gain_grad[:, :128] = value[TAPS : TAPS + 1]
    back = pltpu.roll(value[21:32], 64, 1)
    tap_grad[0:HALF, 128:] = value[21:32, : CH - 128]
    tap_grad[HALF:TAPS, 128:] = back[0 : TAPS - HALF, : CH - 128]
    gain_grad[:, 128:] = back[TAPS - HALF : TAPS - HALF + 1, : CH - 128]


def shape(dims, dtype=F32):
    return jax.ShapeDtypeStruct(dims, dtype)


def swap_near(value):
    return lax.ppermute(value, "xh", [(0, 1), (1, 0)])


def swap_far(value):
    n = 128
    return lax.ppermute(value, GRID, [(i, (i + 1 if i % 2 else i - 1) % n) for i in range(n)])


def per_device(field, cotangent, pre_hidden, w_up, w_down, gain, tap_weights, basis, lon_offsets):
    field = field.reshape(CELLS, CH)
    cot = cotangent.reshape(CELLS, CH)
    pre = pre_hidden.reshape(CELLS, HID)
    place = lax.axis_index(("xh", "chan")).astype(jnp.int32).reshape(1)
    ext_shape = (2, ROWS * EXT, 128)

    slots = call(
        prep_kernel, shape((2 * NCHAN, CH, CELLS), BF16), [SMEM, VMEM, VMEM], VMEM, [], "prep", flops=8_000_000_000, limit=60
    )(place, cot, field)
    line = lax.all_to_all(slots, ("xh", "chan"), 0, 0)
    far = swap_far(field)
    slope, gain_t, taps = call(
        ready_kernel,
        (shape((HID, CELLS)), shape((CH, CELLS)), shape((TAPS, 256))),
        [VMEM] * 3,
        (VMEM,) * 3,
        [],
        "ready",
        moved=3_000_000,
    )(pre, gain.reshape(1, CH), tap_weights)
    part = call(mlp_kernel, shape((D, CELLS), BF16), [SMEM] + [VMEM] * 4, VMEM, [], "mlp", flops=300_000_000)(
        place, line, slope, w_down, w_up
    )
    fwd_t, send, ext = call(
        forward_kernel,
        (shape((CH, CELLS)), shape((SEND, CELLS), BF16), shape(ext_shape)),
        [SMEM] * 3 + [VMEM] * 6,
        (VMEM,) * 3,
        [pltpu.VMEM((CELLS, CH), F32)],
        "forward",
    )(place, lon_offsets, basis, field, line, far, taps, gain_t, part)
    got = lax.all_gather(send, "chan")
    term, term16, packed = call(
        term_kernel,
        (shape((CELLS, CH)), shape((CELLS, CH), BF16), shape((8, PACK, 128), BF16)),
        [SMEM] * 3 + [VMEM] * 4,
        (VMEM,) * 3,
        [pltpu.VMEM((2, 24, 128), F32)],
        "term",
    )(place, lon_offsets, basis, ext, fwd_t, gain_t, got)
    one = lax.all_to_all(packed, "z", 0, 0)
    term_far = swap_far(term)
    one, term_again = lax.optimization_barrier((one, term16))
    again = call(resum_kernel, shape((16, PACK, 128), BF16), [VMEM], VMEM, [], "resum")(one)
    two = lax.all_to_all(again, ("y", "xh"), 0, 0)
    term_near = swap_near(term_again)
    grad = call(
        adjoint_kernel,
        shape((CELLS, CH), BF16),
        [SMEM] * 3 + [VMEM] * 5,
        VMEM,
        [pltpu.VMEM(ext_shape, F32), pltpu.VMEM((CELLS, CH), F32)],
        "adjoint",
        flops=2_000_000_000,
    )(place, lon_offsets, basis, term, term_near, term_far, taps, cot)
    gain_grad, tap_grad = call(
        last_kernel, (shape((1, CH)), shape((TAPS, CH))), [VMEM], (VMEM,) * 2, [], "last"
    )(two)
    return (grad.reshape(ROWS, LON, CH), gain_grad.reshape(CH), tap_grad)


def solution(mesh):
    fine = Mesh(mesh.devices.reshape(8, 8, 2, NCHAN), (*GRID, "chan"))
    cells = P(None, GRID, "chan")
    placed = (
        cells,
        cells,
        cells,
        P(None, "chan"),
        P("chan", None),
        P("chan"),
        P(None, "chan"),
        P(),
        P(),
    )
    return jax.shard_map(
        per_device,
        mesh=fine,
        in_specs=placed,
        out_specs=(cells, P("chan"), P(None, "chan")),
        check_vma=False,
    )
```

```python
import math

import jax
import jax.numpy as jnp
from jax import lax
from jax.experimental import pallas as pl
from jax.experimental.pallas import tpu as pltpu
from jax.sharding import Mesh
from jax.sharding import PartitionSpec as P

ROWS = 16
LON = 8
CELLS = ROWS * LON
D = 768
CH = 192
HID = 768
TAPS = 20
REACH = 2
PER_ROW = 4
NCHAN = 4
EXT = 3 * LON
GRID = ("z", "y", "xh")

EPSILON = 1e-05
INV_SQRT_TWO = 0.7071067811865476
INV_SQRT_TWO_PI = 0.3989422804014327
SCALE = 1.0 / math.sqrt(16384.0)

F32 = jnp.float32
BF16 = jnp.bfloat16
NT = (((1,), (1,)), ((), ()))

FWD_AT = D
SQ_AT = D + CH
SEND = SQ_AT + 16
PACK = 32
HALF = 11

VMEM = pl.BlockSpec(memory_space=pltpu.VMEM)
SMEM = pl.BlockSpec(memory_space=pltpu.SMEM)
HBM = pl.BlockSpec(memory_space=pltpu.HBM)


def call(kernel, outs, ins, out_specs, scratch, name, flops=0, moved=0, limit=24):
    return pl.pallas_call(
        kernel,
        out_shape=outs,
        in_specs=ins,
        out_specs=out_specs,
        scratch_shapes=scratch,
        compiler_params=pltpu.CompilerParams(vmem_limit_bytes=limit * 1024 * 1024),
        cost_estimate=pl.CostEstimate(flops=flops, bytes_accessed=moved, transcendentals=0),
        name=name,
    )


def taps_from(row):
    out = []
    for k in range(TAPS):
        src = row + k // PER_ROW - REACH
        if 0 <= src < ROWS:
            out.append((k, src))
    return out


def fill_own(ext, v):
    for r in range(ROWS):
        to = pl.ds(EXT * r + LON, LON)
        ext[0, to, :] = v[LON * r : LON * r + LON, :128]
        ext[1, to, : CH - 128] = v[LON * r : LON * r + LON, 128:]


def fill_side(ext, v, start):
    for r in range(ROWS):
        to = pl.ds(pl.multiple_of(EXT * r + start, LON), LON)
        ext[0, to, :] = v[LON * r : LON * r + LON, :128]
        ext[1, to, : CH - 128] = v[LON * r : LON * r + LON, 128:]


def fill_ext(ext, place, own, near, far):
    ext[1] = jnp.zeros((ROWS * EXT, 128), F32)
    start = 2 * LON * (1 - (place[0] >> 2))
    fill_own(ext, own)
    fill_side(ext, near, start)
    fill_side(ext, far, 2 * LON - start)


def prep_kernel(place, cot, field, out):
    cot_t = cot[...].astype(F32).T.astype(BF16)
    field_t = field[...].astype(F32).T.astype(BF16)
    x_hi = place[0] >> 2
    for i in range(NCHAN):
        out[NCHAN * x_hi + i] = cot_t
        out[NCHAN * (1 - x_hi) + i] = field_t


def ready_kernel(pre, gain, taps, slope, gain_t, wide):
    v = pre[...].astype(F32)
    s = (
        0.5 * (1.0 + lax.erf(v * INV_SQRT_TWO))
        + v * jnp.exp(-0.5 * v * v) * INV_SQRT_TWO_PI
    )
    slope[...] = s
    gain_t[...] = jnp.broadcast_to(gain[...], (CELLS, CH)).T
    wide[...] = jnp.zeros((TAPS, 256), F32)
    wide[:, :CH] = taps[...]


def mlp_kernel(place, line, slope, down, up, out):
    cot = line[pl.ds(NCHAN * (place[0] >> 2), NCHAN)].reshape(D, CELLS)
    hidden = lax.dot_general(
        cot.astype(F32).T.astype(BF16), down[...], NT, preferred_element_type=F32
    )
    grad = (hidden * slope[...]).astype(BF16)
    out[...] = lax.dot_general(grad, up[...], NT, preferred_element_type=F32).T.astype(BF16)


def forward_kernel(place, offs, basis, own, line, far, taps, gain_t, part, fwd_t, send, ext, fwd):
    x_hi = place[0] >> 2
    near = line[NCHAN * (1 - x_hi) + (place[0] & 3)].astype(F32).T
    fill_ext(ext, place, own[...].astype(F32), near, far[...].astype(F32))
    for r in range(ROWS):
        lo = jnp.zeros((LON, 128), F32)
        hi = jnp.zeros((LON, 128), F32)
        for k, src in taps_from(r):
            at = pl.ds(EXT * src + LON + offs[r, k], LON)
            lo += basis[r, k] * (taps[k : k + 1, :128] * ext[0, at, :])
            hi += basis[r, k] * (taps[k : k + 1, 128:] * ext[1, at, :])
        fwd[LON * r : LON * (r + 1), :128] = lo
        fwd[LON * r : LON * (r + 1), 128:] = hi[:, : CH - 128]
    f = fwd[...].T
    fwd_t[...] = f
    send[:FWD_AT, :] = part[...]
    send[FWD_AT:SQ_AT, :] = (gain_t[...] * f).astype(BF16)
    sq = jnp.sum(f * f, axis=0, keepdims=True)
    top = sq.astype(BF16).astype(F32)
    mid = (sq - top).astype(BF16).astype(F32)
    row = lax.broadcasted_iota(jnp.int32, (16, CELLS), 0)
    three = jnp.where(row == 0, top, jnp.where(row == 1, mid, sq - top - mid))
    send[SQ_AT:, :] = three.astype(BF16)


def term_kernel(place, offs, basis, ext, fwd_t, gain_t, got, term, term16, packed, rows):
    inner = jnp.zeros((1, CELLS), F32)
    squares = jnp.zeros((1, CELLS), F32)
    for j in range(NCHAN):
        norm = got[0, CH * j : CH * (j + 1), :].astype(F32)
        for h in range(1, NCHAN):
            norm += got[h, CH * j : CH * (j + 1), :].astype(F32)
        f = got[j, FWD_AT:SQ_AT, :].astype(F32)
        inner += jnp.sum(f * norm, axis=0, keepdims=True)
        three = got[j, SQ_AT:, :].astype(F32)
        squares += three[0:1] + three[1:2] + three[2:3]
    mine = pl.ds(pl.multiple_of((place[0] & 3) * CH, CH), CH)
    norm = got[0, mine, :].astype(F32)
    for h in range(1, NCHAN):
        norm += got[h, mine, :].astype(F32)
    inv_rms = lax.rsqrt(squares / D + EPSILON)
    f = fwd_t[...]
    scaled = inv_rms * norm
    ft = (gain_t[...] * scaled - f * (inv_rms * inv_rms * inv_rms * (inner / D))).T
    term[...] = ft
    term16[...] = ft.astype(BF16)
    gain_row = jnp.sum((scaled * f).T, axis=0, keepdims=True)
    rows[...] = jnp.zeros((2, 24, 128), F32)
    rows[0, 20:21, :] = gain_row[:, :128]
    rows[1, 20:21, : CH - 128] = gain_row[:, 128:]
    pad = jnp.zeros((LON, 256 - CH), F32)
    for k in range(TAPS):
        lo = jnp.zeros((LON, 128), F32)
        hi = jnp.zeros((LON, 128), F32)
        for r in range(ROWS):
            src = r + k // PER_ROW - REACH
            if 0 <= src < ROWS:
                at = pl.ds(EXT * src + LON + offs[r, k], LON)
                lo += basis[r, k] * (ft[LON * r : LON * (r + 1), :128] * ext[0, at, :])
                wide = jnp.concatenate([ft[LON * r : LON * (r + 1), 128:], pad], axis=1)
                hi += basis[r, k] * (wide * ext[1, at, :])
        rows[0, k : k + 1, :] = jnp.sum(lo, axis=0, keepdims=True)
        rows[1, k : k + 1, :] = jnp.sum(hi, axis=0, keepdims=True)
    first = rows[0, 0:21, :]
    second = rows[1, 0:HALF, :] + pltpu.roll(rows[1, HALF : 2 * HALF, :], 64, 1)
    value = jnp.concatenate([first, second], axis=0).astype(BF16)
    for i in range(8):
        packed[i] = value


def resum_kernel(got, out):
    total = got[0].astype(F32)
    for i in range(1, 8):
        total += got[i].astype(F32)
    total = total.astype(BF16)
    for i in range(16):
        out[i] = total


def adjoint_kernel(place, offs, basis, own, near, far, taps, cot, grad, ext, total):
    fill_ext(ext, place, own[...], near[...].astype(F32), far[...].astype(F32))
    for r2 in range(ROWS):
        lo = jnp.zeros((LON, 128), F32)
        hi = jnp.zeros((LON, 128), F32)
        for k in range(TAPS):
            r = r2 - (k // PER_ROW - REACH)
            if 0 <= r < ROWS:
                at = pl.ds(EXT * r + LON - offs[r, k], LON)
                lo += basis[r, k] * (taps[k : k + 1, :128] * ext[0, at, :])
                hi += basis[r, k] * (taps[k : k + 1, 128:] * ext[1, at, :])
        total[LON * r2 : LON * (r2 + 1), :128] = lo
        total[LON * r2 : LON * (r2 + 1), 128:] = hi[:, : CH - 128]
    grad[...] = (cot[...].astype(F32) + total[...]).astype(BF16)


def last_kernel(got, gain_grad, tap_grad):
    value = got[0].astype(F32)
    for i in range(1, 16):
        value += got[i].astype(F32)
    value = value * SCALE
    tap_grad[:, :128] = value[0:TAPS]
    gain_grad[:, :128] = value[TAPS : TAPS + 1]
    back = pltpu.roll(value[21:32], 64, 1)
    tap_grad[0:HALF, 128:] = value[21:32, : CH - 128]
    tap_grad[HALF:TAPS, 128:] = back[0 : TAPS - HALF, : CH - 128]
    gain_grad[:, 128:] = back[TAPS - HALF : TAPS - HALF + 1, : CH - 128]


def shape(dims, dtype=F32):
    return jax.ShapeDtypeStruct(dims, dtype)


def swap_near(value):
    return lax.ppermute(value, "xh", [(0, 1), (1, 0)])


def swap_far(value):
    n = 128
    return lax.ppermute(value, GRID, [(i, (i + 1 if i % 2 else i - 1) % n) for i in range(n)])


def per_device(field, cotangent, pre_hidden, w_up, w_down, gain, tap_weights, basis, lon_offsets):
    field = field.reshape(CELLS, CH)
    cot = cotangent.reshape(CELLS, CH)
    pre = pre_hidden.reshape(CELLS, HID)
    place = lax.axis_index(("xh", "chan")).astype(jnp.int32).reshape(1)
    ext_shape = (2, ROWS * EXT, 128)

    slots = call(
        prep_kernel, shape((2 * NCHAN, CH, CELLS), BF16), [SMEM, VMEM, VMEM], VMEM, [], "prep", flops=8_000_000_000, limit=60
    )(place, cot, field)
    line = lax.all_to_all(slots, ("xh", "chan"), 0, 0)
    far = swap_far(field)
    slope, gain_t, taps = call(
        ready_kernel,
        (shape((CELLS, HID)), shape((CH, CELLS)), shape((TAPS, 256))),
        [VMEM] * 3,
        (VMEM,) * 3,
        [],
        "ready",
        moved=3_000_000,
    )(pre, gain.reshape(1, CH), tap_weights)
    part = call(mlp_kernel, shape((D, CELLS), BF16), [SMEM] + [VMEM] * 4, VMEM, [], "mlp", flops=300_000_000)(
        place, line, slope, w_down, w_up
    )
    fwd_t, send, ext = call(
        forward_kernel,
        (shape((CH, CELLS)), shape((SEND, CELLS), BF16), shape(ext_shape)),
        [SMEM] * 3 + [VMEM] * 6,
        (VMEM,) * 3,
        [pltpu.VMEM((CELLS, CH), F32)],
        "forward",
    )(place, lon_offsets, basis, field, line, far, taps, gain_t, part)
    got = lax.all_gather(send, "chan")
    term, term16, packed = call(
        term_kernel,
        (shape((CELLS, CH)), shape((CELLS, CH), BF16), shape((8, PACK, 128), BF16)),
        [SMEM] * 3 + [VMEM] * 4,
        (VMEM,) * 3,
        [pltpu.VMEM((2, 24, 128), F32)],
        "term",
    )(place, lon_offsets, basis, ext, fwd_t, gain_t, got)
    one = lax.all_to_all(packed, "z", 0, 0)
    term_far = swap_far(term)
    one, term_again = lax.optimization_barrier((one, term16))
    again = call(resum_kernel, shape((16, PACK, 128), BF16), [VMEM], VMEM, [], "resum")(one)
    two = lax.all_to_all(again, ("y", "xh"), 0, 0)
    term_near = swap_near(term_again)
    grad = call(
        adjoint_kernel,
        shape((CELLS, CH), BF16),
        [SMEM] * 3 + [VMEM] * 5,
        VMEM,
        [pltpu.VMEM(ext_shape, F32), pltpu.VMEM((CELLS, CH), F32)],
        "adjoint",
        flops=2_000_000_000,
    )(place, lon_offsets, basis, term, term_near, term_far, taps, cot)
    gain_grad, tap_grad = call(
        last_kernel, (shape((1, CH)), shape((TAPS, CH))), [VMEM], (VMEM,) * 2, [], "last"
    )(two)
    return (grad.reshape(ROWS, LON, CH), gain_grad.reshape(CH), tap_grad)


def solution(mesh):
    fine = Mesh(mesh.devices.reshape(8, 8, 2, NCHAN), (*GRID, "chan"))
    cells = P(None, GRID, "chan")
    placed = (
        cells,
        cells,
        cells,
        P(None, "chan"),
        P("chan", None),
        P("chan"),
        P(None, "chan"),
        P(),
        P(),
    )
    return jax.shard_map(
        per_device,
        mesh=fine,
        in_specs=placed,
        out_specs=(cells, P("chan"), P(None, "chan")),
        check_vma=False,
    )
```

```python
import math

import jax
import jax.numpy as jnp
from jax import lax
from jax.experimental import pallas as pl
from jax.experimental.pallas import tpu as pltpu
from jax.sharding import Mesh
from jax.sharding import PartitionSpec as P

ROWS = 16
LON = 8
CELLS = ROWS * LON
D = 768
CH = 192
HID = 768
TAPS = 20
REACH = 2
PER_ROW = 4
NCHAN = 4
EXT = 3 * LON
GRID = ("z", "y", "xh")

EPSILON = 1e-05
INV_SQRT_TWO = 0.7071067811865476
INV_SQRT_TWO_PI = 0.3989422804014327
SCALE = 1.0 / math.sqrt(16384.0)

F32 = jnp.float32
BF16 = jnp.bfloat16
NT = (((1,), (1,)), ((), ()))

FWD_AT = D
SQ_AT = D + CH
SEND = SQ_AT + 16
PACK = 32
HALF = 11

VMEM = pl.BlockSpec(memory_space=pltpu.VMEM)
SMEM = pl.BlockSpec(memory_space=pltpu.SMEM)
HBM = pl.BlockSpec(memory_space=pltpu.HBM)


def call(kernel, outs, ins, out_specs, scratch, name, flops=0, moved=0, limit=24):
    return pl.pallas_call(
        kernel,
        out_shape=outs,
        in_specs=ins,
        out_specs=out_specs,
        scratch_shapes=scratch,
        compiler_params=pltpu.CompilerParams(vmem_limit_bytes=limit * 1024 * 1024),
        cost_estimate=pl.CostEstimate(flops=flops, bytes_accessed=moved, transcendentals=0),
        name=name,
    )


def taps_from(row):
    out = []
    for k in range(TAPS):
        src = row + k // PER_ROW - REACH
        if 0 <= src < ROWS:
            out.append((k, src))
    return out


def fill_own(ext, v):
    for r in range(ROWS):
        to = pl.ds(EXT * r + LON, LON)
        ext[0, to, :] = v[LON * r : LON * r + LON, :128]
        ext[1, to, : CH - 128] = v[LON * r : LON * r + LON, 128:]


def fill_side(ext, v, start):
    for r in range(ROWS):
        to = pl.ds(pl.multiple_of(EXT * r + start, LON), LON)
        ext[0, to, :] = v[LON * r : LON * r + LON, :128]
        ext[1, to, : CH - 128] = v[LON * r : LON * r + LON, 128:]


def fill_ext(ext, place, own, near, far):
    ext[1] = jnp.zeros((ROWS * EXT, 128), F32)
    start = 2 * LON * (1 - (place[0] >> 2))
    fill_own(ext, own)
    fill_side(ext, near, start)
    fill_side(ext, far, 2 * LON - start)


def prep_kernel(place, cot, field, out):
    cot_t = cot[...].astype(F32).T.astype(BF16)
    field_t = field[...].astype(F32).T.astype(BF16)
    x_hi = place[0] >> 2
    for i in range(NCHAN):
        out[NCHAN * x_hi + i] = cot_t
        out[NCHAN * (1 - x_hi) + i] = field_t


def ready_kernel(pre, gain, taps, slope, gain_t, wide):
    v = pre[...].astype(F32)
    s = (
        0.5 * (1.0 + lax.erf(v * INV_SQRT_TWO))
        + v * jnp.exp(-0.5 * v * v) * INV_SQRT_TWO_PI
    )
    slope[...] = s
    gain_t[...] = jnp.broadcast_to(gain[...], (CELLS, CH)).T
    wide[...] = jnp.zeros((TAPS, 256), F32)
    wide[:, :CH] = taps[...]


def mlp_kernel(place, line, slope, down, up, out):
    cot = line[pl.ds(NCHAN * (place[0] >> 2), NCHAN)].reshape(D, CELLS)
    hidden = lax.dot_general(
        cot.astype(F32).T.astype(BF16), down[...], NT, preferred_element_type=F32
    )
    grad = (hidden * slope[...]).astype(BF16)
    out[...] = lax.dot_general(grad, up[...], NT, preferred_element_type=F32).T.astype(BF16)


def forward_kernel(place, offs, basis, own, line, far, taps, gain_t, part, fwd_t, send, ext, fwd):
    x_hi = place[0] >> 2
    near = line[NCHAN * (1 - x_hi) + (place[0] & 3)].astype(F32).T
    fill_ext(ext, place, own[...].astype(F32), near, far[...].astype(F32))
    for r in range(ROWS):
        lo = jnp.zeros((LON, 128), F32)
        hi = jnp.zeros((LON, 128), F32)
        for k, src in taps_from(r):
            at = pl.ds(EXT * src + LON + offs[r, k], LON)
            lo += basis[r, k] * (taps[k : k + 1, :128] * ext[0, at, :])
            hi += basis[r, k] * (taps[k : k + 1, 128:] * ext[1, at, :])
        fwd[LON * r : LON * (r + 1), :128] = lo
        fwd[LON * r : LON * (r + 1), 128:] = hi[:, : CH - 128]
    f = fwd[...].T
    fwd_t[...] = f
    send[:FWD_AT, :] = part[...]
    send[FWD_AT:SQ_AT, :] = (gain_t[...] * f).astype(BF16)
    sq = jnp.sum(f * f, axis=0, keepdims=True)
    top = sq.astype(BF16).astype(F32)
    mid = (sq - top).astype(BF16).astype(F32)
    row = lax.broadcasted_iota(jnp.int32, (16, CELLS), 0)
    three = jnp.where(row == 0, top, jnp.where(row == 1, mid, sq - top - mid))
    send[SQ_AT:, :] = three.astype(BF16)


def term_kernel(place, offs, basis, ext, fwd_t, gain_t, got, term, term16, packed, rows):
    inner = jnp.zeros((1, CELLS), F32)
    squares = jnp.zeros((1, CELLS), F32)
    for j in range(NCHAN):
        norm = got[0, CH * j : CH * (j + 1), :].astype(F32)
        for h in range(1, NCHAN):
            norm += got[h, CH * j : CH * (j + 1), :].astype(F32)
        f = got[j, FWD_AT:SQ_AT, :].astype(F32)
        inner += jnp.sum(f * norm, axis=0, keepdims=True)
        three = got[j, SQ_AT:, :].astype(F32)
        squares += three[0:1] + three[1:2] + three[2:3]
    mine = pl.ds(pl.multiple_of((place[0] & 3) * CH, CH), CH)
    norm = got[0, mine, :].astype(F32)
    for h in range(1, NCHAN):
        norm += got[h, mine, :].astype(F32)
    inv_rms = lax.rsqrt(squares / D + EPSILON)
    f = fwd_t[...]
    scaled = inv_rms * norm
    ft = (gain_t[...] * scaled - f * (inv_rms * inv_rms * inv_rms * (inner / D))).T
    term[...] = ft
    term16[...] = ft.astype(BF16)
    gain_row = jnp.sum((scaled * f).T, axis=0, keepdims=True)
    rows[...] = jnp.zeros((2, 24, 128), F32)
    rows[0, 20:21, :] = gain_row[:, :128]
    rows[1, 20:21, : CH - 128] = gain_row[:, 128:]
    pad = jnp.zeros((LON, 256 - CH), F32)
    for k in range(TAPS):
        lo = jnp.zeros((LON, 128), F32)
        hi = jnp.zeros((LON, 128), F32)
        for r in range(ROWS):
            src = r + k // PER_ROW - REACH
            if 0 <= src < ROWS:
                at = pl.ds(EXT * src + LON + offs[r, k], LON)
                lo += basis[r, k] * (ft[LON * r : LON * (r + 1), :128] * ext[0, at, :])
                wide = jnp.concatenate([ft[LON * r : LON * (r + 1), 128:], pad], axis=1)
                hi += basis[r, k] * (wide * ext[1, at, :])
        rows[0, k : k + 1, :] = jnp.sum(lo, axis=0, keepdims=True)
        rows[1, k : k + 1, :] = jnp.sum(hi, axis=0, keepdims=True)
    first = rows[0, 0:21, :]
    second = rows[1, 0:HALF, :] + pltpu.roll(rows[1, HALF : 2 * HALF, :], 64, 1)
    value = jnp.concatenate([first, second], axis=0).astype(BF16)
    for i in range(16):
        packed[i] = value


def resum_kernel(got, out):
    total = got[0].astype(F32)
    for i in range(1, 16):
        total += got[i].astype(F32)
    total = total.astype(BF16)
    for i in range(8):
        out[i] = total


def adjoint_kernel(place, offs, basis, own, near, far, taps, cot, grad, ext, total):
    fill_ext(ext, place, own[...], near[...].astype(F32), far[...].astype(F32))
    for r2 in range(ROWS):
        lo = jnp.zeros((LON, 128), F32)
        hi = jnp.zeros((LON, 128), F32)
        for k in range(TAPS):
            r = r2 - (k // PER_ROW - REACH)
            if 0 <= r < ROWS:
                at = pl.ds(EXT * r + LON - offs[r, k], LON)
                lo += basis[r, k] * (taps[k : k + 1, :128] * ext[0, at, :])
                hi += basis[r, k] * (taps[k : k + 1, 128:] * ext[1, at, :])
        total[LON * r2 : LON * (r2 + 1), :128] = lo
        total[LON * r2 : LON * (r2 + 1), 128:] = hi[:, : CH - 128]
    grad[...] = (cot[...].astype(F32) + total[...]).astype(BF16)


def last_kernel(got, gain_grad, tap_grad):
    value = got[0].astype(F32)
    for i in range(1, 8):
        value += got[i].astype(F32)
    value = value * SCALE
    tap_grad[:, :128] = value[0:TAPS]
    gain_grad[:, :128] = value[TAPS : TAPS + 1]
    back = pltpu.roll(value[21:32], 64, 1)
    tap_grad[0:HALF, 128:] = value[21:32, : CH - 128]
    tap_grad[HALF:TAPS, 128:] = back[0 : TAPS - HALF, : CH - 128]
    gain_grad[:, 128:] = back[TAPS - HALF : TAPS - HALF + 1, : CH - 128]


def shape(dims, dtype=F32):
    return jax.ShapeDtypeStruct(dims, dtype)


def swap_near(value):
    return lax.ppermute(value, "xh", [(0, 1), (1, 0)])


def swap_far(value):
    n = 128
    return lax.ppermute(value, GRID, [(i, (i + 1 if i % 2 else i - 1) % n) for i in range(n)])


def per_device(field, cotangent, pre_hidden, w_up, w_down, gain, tap_weights, basis, lon_offsets):
    field = field.reshape(CELLS, CH)
    cot = cotangent.reshape(CELLS, CH)
    pre = pre_hidden.reshape(CELLS, HID)
    place = lax.axis_index(("xh", "chan")).astype(jnp.int32).reshape(1)
    ext_shape = (2, ROWS * EXT, 128)

    slots = call(
        prep_kernel, shape((2 * NCHAN, CH, CELLS), BF16), [SMEM, VMEM, VMEM], VMEM, [], "prep", flops=8_000_000_000, limit=60
    )(place, cot, field)
    line = lax.all_to_all(slots, ("xh", "chan"), 0, 0)
    far = swap_far(field)
    slope, gain_t, taps = call(
        ready_kernel,
        (shape((CELLS, HID)), shape((CH, CELLS)), shape((TAPS, 256))),
        [VMEM] * 3,
        (VMEM,) * 3,
        [],
        "ready",
        moved=3_000_000,
    )(pre, gain.reshape(1, CH), tap_weights)
    part = call(mlp_kernel, shape((D, CELLS), BF16), [SMEM] + [VMEM] * 4, VMEM, [], "mlp", flops=300_000_000)(
        place, line, slope, w_down, w_up
    )
    fwd_t, send, ext = call(
        forward_kernel,
        (shape((CH, CELLS)), shape((SEND, CELLS), BF16), shape(ext_shape)),
        [SMEM] * 3 + [VMEM] * 6,
        (VMEM,) * 3,
        [pltpu.VMEM((CELLS, CH), F32)],
        "forward",
    )(place, lon_offsets, basis, field, line, far, taps, gain_t, part)
    got = lax.all_gather(send, "chan")
    term, term16, packed = call(
        term_kernel,
        (shape((CELLS, CH)), shape((CELLS, CH), BF16), shape((16, PACK, 128), BF16)),
        [SMEM] * 3 + [VMEM] * 4,
        (VMEM,) * 3,
        [pltpu.VMEM((2, 24, 128), F32)],
        "term",
    )(place, lon_offsets, basis, ext, fwd_t, gain_t, got)
    one = lax.all_to_all(packed, ("y", "xh"), 0, 0)
    term_far = swap_far(term16)
    again = call(resum_kernel, shape((8, PACK, 128), BF16), [VMEM], VMEM, [], "resum")(one)
    two = lax.all_to_all(again, "z", 0, 0)
    term_near = swap_near(term)
    grad = call(
        adjoint_kernel,
        shape((CELLS, CH), BF16),
        [SMEM] * 3 + [VMEM] * 5,
        VMEM,
        [pltpu.VMEM(ext_shape, F32), pltpu.VMEM((CELLS, CH), F32)],
        "adjoint",
        flops=4000000000,
    )(place, lon_offsets, basis, term, term_near, term_far, taps, cot)
    gain_grad, tap_grad = call(
        last_kernel, (shape((1, CH)), shape((TAPS, CH))), [VMEM], (VMEM,) * 2, [], "last"
    )(two)
    return (grad.reshape(ROWS, LON, CH), gain_grad.reshape(CH), tap_grad)


def solution(mesh):
    fine = Mesh(mesh.devices.reshape(8, 8, 2, NCHAN), (*GRID, "chan"))
    cells = P(None, GRID, "chan")
    placed = (
        cells,
        cells,
        cells,
        P(None, "chan"),
        P("chan", None),
        P("chan"),
        P(None, "chan"),
        P(),
        P(),
    )
    return jax.shard_map(
        per_device,
        mesh=fine,
        in_specs=placed,
        out_specs=(cells, P("chan"), P(None, "chan")),
        check_vma=False,
    )
```
